512 devices in a mesh: vis: 64 (over y, z), chan: 8 (over x, core).
Axes of the slice: x: 4, y: 8, z: 8, core: 2. Of those that a mesh axis runs over, the one named last changes fastest.
Arguments:
- model: float32 [2, 256, 1024], P(None, 'vis', 'chan'), may hold values from -6 to 6
- kernels: float32 [2, 32, 8], replicated, may hold values from -1.5 to 1.5
- vis_data: float32 [2, 8, 524288], P(None, 'chan', 'vis'), may hold values from -6 to 6
- vis_weight: float32 [8, 524288], P('chan', 'vis'), may hold values from 0.2 to 2
- tile_list: int32 [8, 64, 16], P('chan', 'vis'), may hold values from 0 to 255, as said below
- vis_slot: int32 [8, 524288], P('chan', 'vis'), may hold values from 0 to 15
- vis_wplane: int32 [8, 524288], P('chan', 'vis'), may hold values from 0 to 31
- vis_offset: int32 [2, 8, 524288], P(None, 'chan', 'vis'), may hold values from 0 to 24
Outputs:
- model_step: float32 [2, 256, 1024], P(None, 'vis', 'chan')
- residual: float32 [2, 8, 524288], P(None, 'chan', 'vis')
The draws below stay inside these ranges and needn't reach their ends.
Inputs may be any that keep to these rules, and one draw needn't show every extreme that they name: `tile_list`: the 16 tiles of one block's list are different and have different owners t // 4.
All inputs are finite; a program needn't handle non-finite values.
Results may differ from the reference program's by a relative error of at most 0.0003.
Values sent between devices are 32-bit elements; how exact they have to be, the bound alone decides.
No kernel may reach another device: no remote copies, remote signals or barrier semaphores. Data moves between devices by JAX's collectives and lax.ppermute only.
A program may use at most 64 MiB of HBM per device.

```python
import math
import jax
import jax.numpy as jnp
from jax import lax

TILE_SIDE = 32
CELLS = 1024
SUPPORT = 8
WPLANES = 32
NTERMS = 2
SLOTS = 16
TILE_DEV = 4
VIS_DEV = 8192
TILES = 256
NVIS = 524288
N_VIS = 64
N_CHAN = 8


def draw_tile_list(key, part):
    key_rank = jax.random.fold_in(key, 11)
    key_score = jax.random.fold_in(key, 12)
    key_within = jax.random.fold_in(key, 13)
    owners = jnp.arange(N_VIS, dtype=jnp.int32)
    order = jax.random.permutation(key_rank, N_VIS).astype(jnp.int32)
    rank = jnp.zeros((N_VIS,), jnp.int32).at[order].set(owners)
    favour = (N_VIS - rank) * 65536 // N_VIS
    noise = jax.random.randint(key_score, (N_CHAN, N_VIS, N_VIS), 0, 65536, dtype=jnp.int32)
    scores = (noise + favour[None, None, :]) * N_VIS + owners[None, None, :]
    first = (jnp.arange(N_CHAN, dtype=jnp.int32)[:, None, None] == 0) & (jnp.arange(N_VIS, dtype=jnp.int32)[None, :, None] == 0)
    forced = first & ((owners[None, None, :] == 0) | (owners[None, None, :] == N_VIS - 1))
    scores = scores + jnp.where(forced, jnp.int32(1 << 28), jnp.int32(0))
    picked = lax.top_k(scores, SLOTS)[1].astype(jnp.int32)
    within = jax.random.randint(key_within, (N_CHAN, N_VIS, SLOTS), 0, TILE_DEV, dtype=jnp.int32)
    first_slots = first[:, :, :1]
    within = jnp.where(first_slots & (picked == 0), jnp.int32(0), within)
    within = jnp.where(first_slots & (picked == N_VIS - 1), jnp.int32(TILE_DEV - 1), within)
    return picked * TILE_DEV + within


def place_ends(array, rng, least, top_value):
    dims = array.shape
    index_at = [jax.random.randint(jax.random.fold_in(rng, axis), (), 0, dims[axis]) for axis in range(len(dims))]
    array = array.at[tuple(index_at)].set(least)
    longest = dims.index(max(dims))
    index_at[longest] = (index_at[longest] + 1) % dims[longest]
    return array.at[tuple(index_at)].set(top_value)


def block_scale(stream_key, shape, shards, smallest, largest):
    level = 1.0
    for dim, shards_of in shards:
        steps = jax.random.uniform(jax.random.fold_in(jax.random.fold_in(stream_key, 6), dim), (shards_of,), jnp.float32, smallest / len(shards), largest / len(shards))
        level = level * jnp.repeat(jnp.exp(steps), shape[dim] // shards_of).reshape((-1,) + (1,) * (len(shape) - 1 - dim))
    return level


def centred(rng, dims, deviation, limit, split=(), kind=jnp.bfloat16):
    array = deviation * jax.random.normal(rng, dims, jnp.float32)
    if split:
        array = array * block_scale(rng, dims, split, -0.22, 0.18)
    return jnp.clip(array, -limit, limit).astype(kind)


def setup_inputs(seed: int = 0) -> dict:
    seeds = jax.random.split(jax.random.key(seed), 9)
    model = centred(seeds[0], (NTERMS, TILES, CELLS), 1.0, 6.0, ((1, 64), (2, 8)), jnp.float32)
    kernels = centred(seeds[1], (2, WPLANES, SUPPORT), 0.25, 1.5, (), jnp.float32)
    vis_data = centred(seeds[2], (2, N_CHAN, NVIS), 1.0, 6.0, ((1, 8), (2, 64)), jnp.float32)
    vis_weight = jnp.clip(jnp.exp(math.log(2.0) - 2.3025851 * jax.random.uniform(seeds[3], (N_CHAN, NVIS), jnp.float32) ** block_scale(seeds[3], (N_CHAN, NVIS), ((0, 8), (1, 64)), -0.2, 0.2)), 0.2, 2.0)
    tile_list = draw_tile_list(jax.random.fold_in(seeds[8], 71), 0)
    vis_slot = place_ends(jax.random.randint(seeds[5], (N_CHAN, NVIS), 0, SLOTS), jax.random.fold_in(seeds[5], 1), 0, SLOTS - 1).astype(jnp.int32)
    vis_wplane = place_ends(jax.random.randint(seeds[6], (N_CHAN, NVIS), 0, WPLANES), jax.random.fold_in(seeds[6], 1), 0, WPLANES - 1).astype(jnp.int32)
    vis_offset = place_ends(jax.random.randint(seeds[7], (2, N_CHAN, NVIS), 0, TILE_SIDE - SUPPORT + 1), jax.random.fold_in(seeds[7], 1), 0, TILE_SIDE - SUPPORT).astype(jnp.int32)
    return {"model": model, "kernels": kernels, "vis_data": vis_data, "vis_weight": vis_weight, "tile_list": tile_list, "vis_slot": vis_slot, "vis_wplane": vis_wplane, "vis_offset": vis_offset}


HIGH = lax.Precision.HIGHEST

def dft_tables(side):
    index = jnp.arange(side, dtype=jnp.int32)
    angle = 2.0 * math.pi / side * (index[:, None] * index[None, :] % side).astype(jnp.float32)
    scale = 1.0 / math.sqrt(side)
    return (jnp.cos(angle) * scale, -jnp.sin(angle) * scale)

def forward(images, cosine, sine):

    def triple(left, right):
        return jnp.einsum('pa,tab,bq->tqp', left, images, right, precision=HIGH)
    return (triple(cosine, cosine) - triple(sine, sine), triple(cosine, sine) + triple(sine, cosine))

def adjoint(part_re, part_im, cosine, sine):

    def triple(left, middle, right):
        return jnp.einsum('ap,tqp,qb->tab', left, middle, right, precision=HIGH)
    return triple(cosine, part_re, cosine) - triple(sine, part_re, sine) + triple(sine, part_im, cosine) + triple(cosine, part_im, sine)

def place(offset, taps, side):
    rows = jnp.arange(side, dtype=jnp.int32)[:, None]
    shift = rows - offset[None, :]
    total = jnp.zeros((side, offset.shape[0]), jnp.float32)
    for tap in range(taps.shape[0]):
        total = total + jnp.where(shift == tap, taps[tap][None, :], jnp.float32(0.0))
    return total

def crossed(left, right):
    return lax.dot_general(left, right, (((1,), (1,)), ((), ())), precision=HIGH)

def visibility_pass(grid_re, grid_im, slot, wplane, off_u, off_v, data_re, data_im, weight, kernels):
    slots, side = (grid_re.shape[0], grid_re.shape[1])
    planes = kernels.shape[1]
    picker = (jnp.arange(planes, dtype=jnp.int32)[:, None] == wplane[None, :]).astype(jnp.float32)
    taps_re = jnp.dot(kernels[0].T, picker, precision=HIGH)
    taps_im = jnp.dot(kernels[1].T, picker, precision=HIGH)
    a_re = place(off_u, taps_re, side)
    a_im = place(off_u, taps_im, side)
    b_re = place(off_v, taps_re, side)
    b_im = place(off_v, taps_im, side)
    flat_re = grid_re.reshape(slots * side, side)
    flat_im = grid_im.reshape(slots * side, side)
    y_re = jnp.dot(flat_re, a_re, precision=HIGH) - jnp.dot(flat_im, a_im, precision=HIGH)
    y_im = jnp.dot(flat_re, a_im, precision=HIGH) + jnp.dot(flat_im, a_re, precision=HIGH)
    y_re = y_re.reshape(slots, side, -1)
    y_im = y_im.reshape(slots, side, -1)
    owner = (jnp.arange(slots, dtype=jnp.int32)[:, None] == slot[None, :]).astype(jnp.float32)
    pred_re = lax.optimization_barrier(jnp.sum(owner * lax.optimization_barrier(jnp.sum(y_re * b_re[None] - y_im * b_im[None], axis=1)), axis=0))
    pred_im = lax.optimization_barrier(jnp.sum(owner * lax.optimization_barrier(jnp.sum(y_re * b_im[None] + y_im * b_re[None], axis=1)), axis=0))
    res_re = weight * (data_re - pred_re)
    res_im = weight * (data_im - pred_im)
    z_re = (owner[:, None, :] * (res_re * b_re + res_im * b_im)[None]).reshape(slots * side, -1)
    z_im = (owner[:, None, :] * (res_im * b_re - res_re * b_im)[None]).reshape(slots * side, -1)
    part_re = crossed(z_re, a_re) + crossed(z_im, a_im)
    part_im = crossed(z_im, a_re) - crossed(z_re, a_im)
    return (res_re, res_im, part_re.reshape(slots, side, side), part_im.reshape(slots, side, side))

def reference(model, kernels, vis_data, vis_weight, tile_list, vis_slot, vis_wplane, vis_offset):
    side = TILE_SIDE
    cells = side * side
    offsets_all = (jnp.arange(N_CHAN, dtype=jnp.float32) - 0.5 * (N_CHAN - 1)) / N_CHAN
    cosine, sine = dft_tables(side)
    count = VIS_DEV
    grad_zero = jnp.zeros((TILES, cells), jnp.float32)
    grad_one = jnp.zeros((TILES, cells), jnp.float32)
    collected = []
    for channel in range(N_CHAN):
        frequency = offsets_all[channel]
        image = (model[0] + frequency * model[1]).reshape(TILES, side, side)
        full_re, full_im = forward(image, cosine, sine)

        def one_block(carry, inputs):
            listed, slot, wplane, off_u, off_v, data_re, data_im, weight = inputs
            res_re, res_im, part_re, part_im = visibility_pass(full_re[listed], full_im[listed], slot, wplane, off_u, off_v, data_re, data_im, weight, kernels)
            return ((carry[0].at[listed].add(part_re), carry[1].at[listed].add(part_im)), (res_re, res_im))
        empty = jnp.zeros((TILES, side, side), jnp.float32)
        sequence = (tile_list[channel], vis_slot[channel].reshape(N_VIS, count), vis_wplane[channel].reshape(N_VIS, count), vis_offset[0, channel].reshape(N_VIS, count), vis_offset[1, channel].reshape(N_VIS, count), vis_data[0, channel].reshape(N_VIS, count), vis_data[1, channel].reshape(N_VIS, count), vis_weight[channel].reshape(N_VIS, count))
        (total_re, total_im), (out_re, out_im) = lax.scan(one_block, (empty, empty), sequence)
        dirty = adjoint(total_re, total_im, cosine, sine).reshape(TILES, cells)
        grad_zero = grad_zero + dirty
        grad_one = grad_one + frequency * dirty
        collected.append(jnp.stack([out_re.reshape(-1), out_im.reshape(-1)]))
    residual = jnp.stack(collected, axis=1)
    model_step = jnp.stack([grad_zero / N_CHAN, grad_one / jnp.sum(offsets_all * offsets_all)])
    return (model_step, residual)
```

```python
import math

import jax
import jax.numpy as jnp
import numpy as np
from jax import lax
from jax.experimental import pallas as pl
from jax.experimental.pallas import tpu as pltpu
from jax.sharding import PartitionSpec as P

SIDE = 32
LANES = 128
SLOTS = 16
OWNERS = 64
CHANS = 8
WITHIN = 4
CHUNK = 256
UNROLL = 2

F32 = jnp.float32
BF16 = jnp.bfloat16


def phase_tables():
    index = np.arange(SIDE)
    turn = np.zeros((SIDE, LANES), np.int64)
    turn[:, :SIDE] = index[:, None] * index[None, :] % SIDE
    angle = 2.0 * np.pi / SIDE * turn
    return np.stack([np.cos(angle), -np.sin(angle)]).astype(np.float32)


def split(x):
    high = x.astype(BF16)
    return high, (x - high.astype(F32)).astype(BF16)


def visibility_kernel(
    image_ref, taps_ref, phase_ref, slot_ref, plane_ref, offset_ref, data_ref, weight_ref,
    residual_ref, dirty_ref, grid_ref, total_ref, table_ref,
):
    rows = slot_ref.shape[0]
    scale = 1.0 / math.sqrt(SIDE)
    cos_s = phase_ref[0][:, :8] * scale
    sin_s = phase_ref[1][:, :8] * scale

    def tapped(table, taps):
        return lax.dot_general(
            table, taps, (((1,), (1,)), ((), ())),
            precision=lax.Precision.HIGHEST, preferred_element_type=F32,
        )

    k_re = tapped(cos_s, taps_ref[0]) - tapped(sin_s, taps_ref[1])
    k_im = tapped(cos_s, taps_ref[1]) + tapped(sin_s, taps_ref[0])
    table_ref[0] = jnp.concatenate([k_re] * 4, axis=1)
    table_ref[1] = jnp.concatenate([k_im] * 4, axis=1)

    for low in range(4):
        tiles = [image_ref[pl.ds(high * 4 + low, 8, stride=SLOTS), :] for high in range(4)]
        for step in range(4):
            grid_ref[pl.ds(low * SIDE + step, 8, stride=4), :] = jnp.concatenate(
                [t[:, step * SIDE : (step + 1) * SIDE] for t in tiles], axis=1
            )
    turned = grid_ref[...].T
    t_high, t_low = split(turned)
    left = jnp.concatenate(
        [jnp.concatenate([t_high, t_high], axis=1), jnp.concatenate([t_low, t_low], axis=1)],
        axis=0,
    )
    total_ref[...] = jnp.zeros_like(total_ref)

    def spread(x, masks):
        high, low = split(x)
        return jnp.concatenate([high * m for m in masks] + [low * m for m in masks], axis=0)

    def masks_of(part):
        return [
            jnp.broadcast_to(jnp.where(part == k, F32(1), F32(0)), (SIDE, LANES)).astype(BF16)
            for k in range(4)
        ]

    def take(table, index):
        return jnp.take_along_axis(table, index, axis=1, mode="promise_in_bounds")

    per_chunk = CHUNK // LANES

    def one_chunk(first):
        lefts_re, lefts_im, rights, masks_high, highs = [], [], [], [], []
        for t in range(per_chunk):
            row = first + t
            slot = slot_ref[pl.ds(row, 1), :]
            plane = jnp.broadcast_to(plane_ref[pl.ds(row, 1), :], (SIDE, LANES))
            u0 = jnp.broadcast_to(offset_ref[0, pl.ds(row, 1), :], (SIDE, LANES))
            v0 = jnp.broadcast_to(offset_ref[1, pl.ds(row, 1), :], (SIDE, LANES))
            w_re, w_im = take(table_ref[0], plane), take(table_ref[1], plane)
            e_re, e_im = take(phase_ref[0], u0), take(phase_ref[1], u0)
            f_re, f_im = take(phase_ref[0], v0), take(phase_ref[1], v0)
            low_masks = masks_of(slot & 3)
            high = slot >> 2
            lefts_re.append(spread(w_re * e_re - w_im * e_im, low_masks))
            lefts_im.append(spread(w_re * e_im + w_im * e_re, low_masks))
            rights.append((w_re * f_re - w_im * f_im, w_re * f_im + w_im * f_re))
            highs.append(jnp.broadcast_to(high, (SIDE, LANES)))
            masks_high.append(masks_of(high))
        a_re = jnp.concatenate(lefts_re, axis=1)
        a_im = jnp.concatenate(lefts_im, axis=1)
        y_re = jnp.dot(left, a_re, preferred_element_type=F32)
        y_im = jnp.dot(left, a_im, preferred_element_type=F32)

        def chosen(y, t):
            y = y[:, t * LANES : (t + 1) * LANES]
            y = y[: 4 * SIDE] + y[4 * SIDE :]
            parts = [y[k * SIDE : (k + 1) * SIDE] for k in range(4)]
            upper = jnp.where(highs[t] == 3, parts[3], parts[2])
            lower = jnp.where(highs[t] == 1, parts[1], parts[0])
            return jnp.where(highs[t] >= 2, upper, lower)

        z_re_all, z_im_all = [], []
        for t in range(per_chunk):
            row = first + t
            b_re, b_im = rights[t]
            p_re, p_im = chosen(y_re, t), chosen(y_im, t)
            pred_re = jnp.sum(p_re * b_re - p_im * b_im, axis=0, keepdims=True)
            pred_im = jnp.sum(p_re * b_im + p_im * b_re, axis=0, keepdims=True)
            weight = weight_ref[pl.ds(row, 1), :]
            r_re = weight * (data_ref[0, pl.ds(row, 1), :] - pred_re)
            r_im = weight * (data_ref[1, pl.ds(row, 1), :] - pred_im)
            residual_ref[0, pl.ds(row, 1), :] = r_re
            residual_ref[1, pl.ds(row, 1), :] = r_im
            z_re_all.append(spread(r_re * b_re + r_im * b_im, masks_high[t]))
            z_im_all.append(spread(r_im * b_re - r_re * b_im, masks_high[t]))

        def crossed(x, y):
            return lax.dot_general(
                x, y, (((1,), (1,)), ((), ())), preferred_element_type=F32
            )

        return crossed(a_re, jnp.concatenate(z_re_all, axis=1)) + crossed(
            a_im, jnp.concatenate(z_im_all, axis=1)
        )

    def step(i, _):
        part = None
        for k in range(UNROLL):
            more = one_chunk((i * UNROLL + k) * per_chunk)
            part = more if part is None else part + more
        total_ref[...] += part
        return 0

    lax.fori_loop(0, rows // (per_chunk * UNROLL), step, 0)

    total = total_ref[...]
    total = total[:, : 4 * SIDE] + total[:, 4 * SIDE :]
    grid_ref[...] = total[: 4 * SIDE] + total[4 * SIDE :]
    for low in range(4):
        parts = [grid_ref[pl.ds(low * SIDE + s, 8, stride=4), :] for s in range(4)]
        for high in range(4):
            dirty_ref[pl.ds(high * 4 + low, 8, stride=SLOTS), :] = jnp.concatenate(
                [p[:, high * SIDE : (high + 1) * SIDE] for p in parts], axis=1
            )


def visibilities(image, kernels, slot, plane, offset, data, weight):
    rows = slot.shape[0]
    return pl.pallas_call(
        visibility_kernel,
        out_shape=(
            jax.ShapeDtypeStruct((2, rows, LANES), F32),
            jax.ShapeDtypeStruct((CHANS * SLOTS, LANES), F32),
        ),
        in_specs=[pl.BlockSpec(memory_space=pltpu.VMEM)] * 8,
        out_specs=(pl.BlockSpec(memory_space=pltpu.VMEM),) * 2,
        scratch_shapes=[
            pltpu.VMEM((LANES, LANES), F32),
            pltpu.VMEM((2 * LANES, 2 * LANES), F32),
            pltpu.VMEM((2, SIDE, LANES), F32),
        ],
        compiler_params=pltpu.CompilerParams(vmem_limit_bytes=32 * 1024 * 1024),
        name="visibilities",
    )(image, kernels, jnp.asarray(phase_tables()), slot, plane, offset, data, weight)


def frequency(channel):
    return (channel.astype(F32) - 0.5 * (CHANS - 1)) / CHANS


def select_kernel(list_ref, model_ref, image_ref):
    for channel in range(CHANS):
        offset = (channel - 0.5 * (CHANS - 1)) / CHANS
        for slot in range(SLOTS):
            tile = list_ref[channel, slot]
            first = (tile // WITHIN) * (2 * WITHIN) + tile % WITHIN
            image_ref[pl.ds(channel * SLOTS + slot, 1), :] = model_ref[
                pl.ds(first, 1), :
            ] + offset * model_ref[pl.ds(first + WITHIN, 1), :]


def select(listed, model):
    return pl.pallas_call(
        select_kernel,
        out_shape=jax.ShapeDtypeStruct((CHANS * SLOTS, LANES), F32),
        in_specs=[
            pl.BlockSpec(memory_space=pltpu.SMEM),
            pl.BlockSpec(memory_space=pltpu.VMEM),
        ],
        out_specs=pl.BlockSpec(memory_space=pltpu.VMEM),
        name="select",
    )(listed, model)


def collect_kernel(list_ref, dirty_ref, owned_ref):
    owned_ref[...] = jnp.zeros_like(owned_ref)
    for channel in range(CHANS):
        offset = (channel - 0.5 * (CHANS - 1)) / CHANS
        for slot in range(SLOTS):
            tile = list_ref[channel, slot]
            first = (tile // WITHIN) * (2 * WITHIN) + tile % WITHIN
            row = dirty_ref[pl.ds(channel * SLOTS + slot, 1), :]
            owned_ref[pl.ds(first, 1), :] += row
            owned_ref[pl.ds(first + WITHIN, 1), :] += offset * row


def collect(listed, dirty):
    return pl.pallas_call(
        collect_kernel,
        out_shape=jax.ShapeDtypeStruct((OWNERS * 2 * WITHIN, LANES), F32),
        in_specs=[
            pl.BlockSpec(memory_space=pltpu.SMEM),
            pl.BlockSpec(memory_space=pltpu.VMEM),
        ],
        out_specs=pl.BlockSpec(memory_space=pltpu.VMEM),
        name="collect",
    )(listed, dirty)


def shards(model, kernels, vis_data, vis_weight, tile_list, vis_slot, vis_wplane, vis_offset):
    count = vis_weight.shape[1]
    rows = count // LANES
    with jax.named_scope("lists"):
        listed = lax.all_to_all(
            jnp.broadcast_to(tile_list.reshape(1, SLOTS), (CHANS, SLOTS)),
            "chan", 0, 0, tiled=True,
        )
    with jax.named_scope("spread_model"):
        own = model.reshape(1, 2 * WITHIN, LANES)
        every = lax.all_to_all(
            jnp.broadcast_to(own, (OWNERS, 2 * WITHIN, LANES)), "vis", 0, 0, tiled=True
        )
    chosen = select(listed, every.reshape(OWNERS * 2 * WITHIN, LANES))
    with jax.named_scope("images"):
        image = lax.all_to_all(chosen, "chan", 0, 0, tiled=True)
    residual, dirty = visibilities(
        image,
        kernels,
        vis_slot.reshape(rows, LANES),
        vis_wplane.reshape(rows, LANES),
        vis_offset.reshape(2, rows, LANES),
        vis_data.reshape(2, rows, LANES),
        vis_weight.reshape(rows, LANES),
    )
    with jax.named_scope("dirty_cells"):
        pieces = lax.all_to_all(dirty, "chan", 0, 0, tiled=True)
    owned = collect(listed, pieces)
    with jax.named_scope("owners"):
        summed = lax.all_to_all(
            owned.reshape(OWNERS, 2 * WITHIN, LANES), "vis", 0, 0, tiled=True
        )
    gradient = jnp.sum(summed, axis=0).reshape(2, WITHIN, LANES)
    offsets = (np.arange(CHANS) - 0.5 * (CHANS - 1)) / CHANS
    curvature = np.array([CHANS, np.sum(offsets * offsets)], np.float32)
    model_step = gradient / curvature[:, None, None]
    return (model_step, residual.reshape(2, 1, count))


def solution(mesh):
    placed = (
        P(None, "vis", "chan"),
        P(),
        P(None, "chan", "vis"),
        P("chan", "vis"),
        P("chan", "vis", None),
        P("chan", "vis"),
        P("chan", "vis"),
        P(None, "chan", "vis"),
    )
    return jax.shard_map(
        shards,
        mesh=mesh,
        in_specs=placed,
        out_specs=(P(None, "vis", "chan"), P(None, "chan", "vis")),
        check_vma=False,
    )
```

```python
import math

import jax
import jax.numpy as jnp
import numpy as np
from jax import lax
from jax.experimental import pallas as pl
from jax.experimental.pallas import tpu as pltpu
from jax.sharding import PartitionSpec as P

SIDE = 32
LANES = 128
SLOTS = 16
OWNERS = 64
CHANS = 8
WITHIN = 4
CHUNK = 512
UNROLL = 4

F32 = jnp.float32
BF16 = jnp.bfloat16


def phase_tables():
    index = np.arange(SIDE)
    turn = np.zeros((SIDE, LANES), np.int64)
    turn[:, :SIDE] = index[:, None] * index[None, :] % SIDE
    angle = 2.0 * np.pi / SIDE * turn
    return np.stack([np.cos(angle), -np.sin(angle)]).astype(np.float32)


def split(x):
    high = x.astype(BF16)
    return high, (x - high.astype(F32)).astype(BF16)


def visibility_kernel(
    image_ref, taps_ref, phase_ref, slot_ref, plane_ref, offset_ref, data_ref, weight_ref,
    residual_ref, dirty_ref, grid_ref, total_ref, table_ref,
):
    rows = slot_ref.shape[0]
    scale = 1.0 / math.sqrt(SIDE)
    cos_s = phase_ref[0][:, :8] * scale
    sin_s = phase_ref[1][:, :8] * scale

    def tapped(table, taps):
        return lax.dot_general(
            table, taps, (((1,), (1,)), ((), ())),
            precision=lax.Precision.HIGHEST, preferred_element_type=F32,
        )

    k_re = tapped(cos_s, taps_ref[0]) - tapped(sin_s, taps_ref[1])
    k_im = tapped(cos_s, taps_ref[1]) + tapped(sin_s, taps_ref[0])
    table_ref[0] = jnp.concatenate([k_re] * 4, axis=1)
    table_ref[1] = jnp.concatenate([k_im] * 4, axis=1)

    for low in range(4):
        tiles = [image_ref[pl.ds(high * 4 + low, 8, stride=SLOTS), :] for high in range(4)]
        for step in range(4):
            grid_ref[pl.ds(low * SIDE + step, 8, stride=4), :] = jnp.concatenate(
                [t[:, step * SIDE : (step + 1) * SIDE] for t in tiles], axis=1
            )
    turned = grid_ref[...].T
    t_high, t_low = split(turned)
    left = jnp.concatenate(
        [jnp.concatenate([t_high, t_high], axis=1), jnp.concatenate([t_low, t_low], axis=1)],
        axis=0,
    )
    total_ref[...] = jnp.zeros_like(total_ref)

    def spread(x, masks):
        high, low = split(x)
        return jnp.concatenate([high * m for m in masks] + [low * m for m in masks], axis=0)

    def masks_of(part):
        return [
            jnp.broadcast_to(jnp.where(part == k, F32(1), F32(0)), (SIDE, LANES)).astype(BF16)
            for k in range(4)
        ]

    def take(table, index):
        return jnp.take_along_axis(table, index, axis=1, mode="promise_in_bounds")

    per_chunk = CHUNK // LANES

    def one_chunk(first):
        lefts_re, lefts_im, rights, masks_high, highs = [], [], [], [], []
        for t in range(per_chunk):
            row = first + t
            slot = slot_ref[pl.ds(row, 1), :]
            plane = jnp.broadcast_to(plane_ref[pl.ds(row, 1), :], (SIDE, LANES))
            u0 = jnp.broadcast_to(offset_ref[0, pl.ds(row, 1), :], (SIDE, LANES))
            v0 = jnp.broadcast_to(offset_ref[1, pl.ds(row, 1), :], (SIDE, LANES))
            w_re, w_im = take(table_ref[0], plane), take(table_ref[1], plane)
            e_re, e_im = take(phase_ref[0], u0), take(phase_ref[1], u0)
            f_re, f_im = take(phase_ref[0], v0), take(phase_ref[1], v0)
            low_masks = masks_of(slot & 3)
            high = slot >> 2
            lefts_re.append(spread(w_re * e_re - w_im * e_im, low_masks))
            lefts_im.append(spread(w_re * e_im + w_im * e_re, low_masks))
            rights.append((w_re * f_re - w_im * f_im, w_re * f_im + w_im * f_re))
            highs.append(jnp.broadcast_to(high, (SIDE, LANES)))
            masks_high.append(masks_of(high))
        a_re = jnp.concatenate(lefts_re, axis=1)
        a_im = jnp.concatenate(lefts_im, axis=1)
        y_re = jnp.dot(left, a_re, preferred_element_type=F32)
        y_im = jnp.dot(left, a_im, preferred_element_type=F32)

        def chosen(y, t):
            y = y[:, t * LANES : (t + 1) * LANES]
            y = y[: 4 * SIDE] + y[4 * SIDE :]
            parts = [y[k * SIDE : (k + 1) * SIDE] for k in range(4)]
            upper = jnp.where(highs[t] == 3, parts[3], parts[2])
            lower = jnp.where(highs[t] == 1, parts[1], parts[0])
            return jnp.where(highs[t] >= 2, upper, lower)

        z_re_all, z_im_all = [], []
        for t in range(per_chunk):
            row = first + t
            b_re, b_im = rights[t]
            p_re, p_im = chosen(y_re, t), chosen(y_im, t)
            pred_re = jnp.sum(p_re * b_re - p_im * b_im, axis=0, keepdims=True)
            pred_im = jnp.sum(p_re * b_im + p_im * b_re, axis=0, keepdims=True)
            weight = weight_ref[pl.ds(row, 1), :]
            r_re = weight * (data_ref[0, pl.ds(row, 1), :] - pred_re)
            r_im = weight * (data_ref[1, pl.ds(row, 1), :] - pred_im)
            residual_ref[0, pl.ds(row, 1), :] = r_re
            residual_ref[1, pl.ds(row, 1), :] = r_im
            z_re_all.append(spread(r_re * b_re + r_im * b_im, masks_high[t]))
            z_im_all.append(spread(r_im * b_re - r_re * b_im, masks_high[t]))

        def crossed(x, y):
            return lax.dot_general(
                x, y, (((1,), (1,)), ((), ())), preferred_element_type=F32
            )

        return crossed(a_re, jnp.concatenate(z_re_all, axis=1)) + crossed(
            a_im, jnp.concatenate(z_im_all, axis=1)
        )

    def step(i, _):
        part = None
        for k in range(UNROLL):
            more = one_chunk((i * UNROLL + k) * per_chunk)
            part = more if part is None else part + more
        total_ref[...] += part
        return 0

    lax.fori_loop(0, rows // (per_chunk * UNROLL), step, 0)

    total = total_ref[...]
    total = total[:, : 4 * SIDE] + total[:, 4 * SIDE :]
    grid_ref[...] = total[: 4 * SIDE] + total[4 * SIDE :]
    for low in range(4):
        parts = [grid_ref[pl.ds(low * SIDE + s, 8, stride=4), :] for s in range(4)]
        for high in range(4):
            dirty_ref[pl.ds(high * 4 + low, 8, stride=SLOTS), :] = jnp.concatenate(
                [p[:, high * SIDE : (high + 1) * SIDE] for p in parts], axis=1
            )


def visibilities(image, kernels, slot, plane, offset, data, weight):
    rows = slot.shape[0]
    return pl.pallas_call(
        visibility_kernel,
        out_shape=(
            jax.ShapeDtypeStruct((2, rows, LANES), F32),
            jax.ShapeDtypeStruct((CHANS * SLOTS, LANES), F32),
        ),
        in_specs=[pl.BlockSpec(memory_space=pltpu.VMEM)] * 8,
        out_specs=(pl.BlockSpec(memory_space=pltpu.VMEM),) * 2,
        scratch_shapes=[
            pltpu.VMEM((LANES, LANES), F32),
            pltpu.VMEM((2 * LANES, 2 * LANES), F32),
            pltpu.VMEM((2, SIDE, LANES), F32),
        ],
        compiler_params=pltpu.CompilerParams(vmem_limit_bytes=32 * 1024 * 1024),
        name="visibilities",
    )(image, kernels, jnp.asarray(phase_tables()), slot, plane, offset, data, weight)


def frequency(channel):
    return (channel.astype(F32) - 0.5 * (CHANS - 1)) / CHANS


def select_kernel(list_ref, model_ref, image_ref):
    for channel in range(CHANS):
        offset = (channel - 0.5 * (CHANS - 1)) / CHANS
        for slot in range(SLOTS):
            tile = list_ref[channel, slot]
            first = (tile // WITHIN) * (2 * WITHIN) + tile % WITHIN
            image_ref[pl.ds(channel * SLOTS + slot, 1), :] = model_ref[
                pl.ds(first, 1), :
            ] + offset * model_ref[pl.ds(first + WITHIN, 1), :]


def select(listed, model):
    return pl.pallas_call(
        select_kernel,
        out_shape=jax.ShapeDtypeStruct((CHANS * SLOTS, LANES), F32),
        in_specs=[
            pl.BlockSpec(memory_space=pltpu.SMEM),
            pl.BlockSpec(memory_space=pltpu.VMEM),
        ],
        out_specs=pl.BlockSpec(memory_space=pltpu.VMEM),
        name="select",
    )(listed, model)


def collect_kernel(list_ref, dirty_ref, owned_ref):
    owned_ref[...] = jnp.zeros_like(owned_ref)
    for channel in range(CHANS):
        offset = (channel - 0.5 * (CHANS - 1)) / CHANS
        for slot in range(SLOTS):
            tile = list_ref[channel, slot]
            first = (tile // WITHIN) * (2 * WITHIN) + tile % WITHIN
            row = dirty_ref[pl.ds(channel * SLOTS + slot, 1), :]
            owned_ref[pl.ds(first, 1), :] += row
            owned_ref[pl.ds(first + WITHIN, 1), :] += offset * row


def collect(listed, dirty):
    return pl.pallas_call(
        collect_kernel,
        out_shape=jax.ShapeDtypeStruct((OWNERS * 2 * WITHIN, LANES), F32),
        in_specs=[
            pl.BlockSpec(memory_space=pltpu.SMEM),
            pl.BlockSpec(memory_space=pltpu.VMEM),
        ],
        out_specs=pl.BlockSpec(memory_space=pltpu.VMEM),
        name="collect",
    )(listed, dirty)


def shards(model, kernels, vis_data, vis_weight, tile_list, vis_slot, vis_wplane, vis_offset):
    count = vis_weight.shape[1]
    rows = count // LANES
    with jax.named_scope("lists"):
        listed = lax.all_gather(tile_list.reshape(1, SLOTS), "chan", axis=0, tiled=True)
    with jax.named_scope("spread_model"):
        own = model.reshape(1, 2 * WITHIN, LANES)
        every = lax.all_to_all(
            jnp.broadcast_to(own, (OWNERS, 2 * WITHIN, LANES)), "vis", 0, 0, tiled=True
        )
    chosen = select(listed, every.reshape(OWNERS * 2 * WITHIN, LANES))
    with jax.named_scope("images"):
        image = lax.all_to_all(chosen, "chan", 0, 0, tiled=True)
    residual, dirty = visibilities(
        image,
        kernels,
        vis_slot.reshape(rows, LANES),
        vis_wplane.reshape(rows, LANES),
        vis_offset.reshape(2, rows, LANES),
        vis_data.reshape(2, rows, LANES),
        vis_weight.reshape(rows, LANES),
    )
    with jax.named_scope("dirty_cells"):
        pieces = lax.all_to_all(dirty, "chan", 0, 0, tiled=True)
    owned = collect(listed, pieces)
    with jax.named_scope("owners"):
        summed = lax.all_to_all(
            owned.reshape(OWNERS, 2 * WITHIN, LANES), "vis", 0, 0, tiled=True
        )
    offsets = (np.arange(CHANS) - 0.5 * (CHANS - 1)) / CHANS
    term = lax.broadcasted_iota(jnp.int32, (2, WITHIN, LANES), 0)
    inverse = jnp.where(term == 0, F32(1.0 / CHANS), F32(1.0 / np.sum(offsets * offsets)))
    model_step = jnp.sum(summed, axis=0).reshape(2, WITHIN, LANES) * inverse
    return (model_step, residual.reshape(2, 1, count))


def solution(mesh):
    placed = (
        P(None, "vis", "chan"),
        P(),
        P(None, "chan", "vis"),
        P("chan", "vis"),
        P("chan", "vis", None),
        P("chan", "vis"),
        P("chan", "vis"),
        P(None, "chan", "vis"),
    )
    return jax.shard_map(
        shards,
        mesh=mesh,
        in_specs=placed,
        out_specs=(P(None, "vis", "chan"), P(None, "chan", "vis")),
        check_vma=False,
    )
```

```python
import math

import jax
import jax.numpy as jnp
import numpy as np
from jax import lax
from jax.experimental import pallas as pl
from jax.experimental.pallas import tpu as pltpu
from jax.sharding import PartitionSpec as P

SIDE = 32
LANES = 128
SLOTS = 16
OWNERS = 64
CHANS = 8
WITHIN = 4
CHUNK = 512

F32 = jnp.float32
BF16 = jnp.bfloat16


def phase_tables():
    index = np.arange(SIDE)
    turn = np.zeros((SIDE, LANES), np.int64)
    turn[:, :SIDE] = index[:, None] * index[None, :] % SIDE
    angle = 2.0 * np.pi / SIDE * turn
    return np.stack([np.cos(angle), -np.sin(angle)]).astype(np.float32)


def split(x):
    high = x.astype(BF16)
    return high, (x - high.astype(F32)).astype(BF16)


def visibility_kernel(
    image_ref, table_ref, phase_ref, slot_ref, plane_ref, offset_ref, data_ref, weight_ref,
    residual_ref, dirty_ref, grid_ref,
):
    rows = slot_ref.shape[0]
    for low in range(4):
        tiles = [image_ref[pl.ds(high * 4 + low, 8, stride=SLOTS), :] for high in range(4)]
        for step in range(4):
            grid_ref[pl.ds(low * SIDE + step, 8, stride=4), :] = jnp.concatenate(
                [t[:, step * SIDE : (step + 1) * SIDE] for t in tiles], axis=1
            )
    turned = grid_ref[...].T
    t_high, t_low = split(turned)
    left = jnp.concatenate(
        [jnp.concatenate([t_high, t_high], axis=1), jnp.concatenate([t_low, t_low], axis=1)],
        axis=0,
    )

    def spread(x, masks):
        high, low = split(x)
        return jnp.concatenate([high * m for m in masks] + [low * m for m in masks], axis=0)

    def masks_of(part):
        return [
            jnp.broadcast_to(jnp.where(part == k, F32(1), F32(0)), (SIDE, LANES)).astype(BF16)
            for k in range(4)
        ]

    def take(table, index):
        return jnp.take_along_axis(table, index, axis=1, mode="promise_in_bounds")

    per_chunk = CHUNK // LANES

    def one_chunk(first):
        lefts_re, lefts_im, rights, masks_high, highs = [], [], [], [], []
        for t in range(per_chunk):
            row = first + t
            slot = slot_ref[pl.ds(row, 1), :]
            plane = jnp.broadcast_to(plane_ref[pl.ds(row, 1), :], (SIDE, LANES))
            u0 = jnp.broadcast_to(offset_ref[0, pl.ds(row, 1), :], (SIDE, LANES))
            v0 = jnp.broadcast_to(offset_ref[1, pl.ds(row, 1), :], (SIDE, LANES))
            w_re, w_im = take(table_ref[0], plane), take(table_ref[1], plane)
            e_re, e_im = take(phase_ref[0], u0), take(phase_ref[1], u0)
            f_re, f_im = take(phase_ref[0], v0), take(phase_ref[1], v0)
            low_masks = masks_of(slot & 3)
            high = slot >> 2
            lefts_re.append(spread(w_re * e_re - w_im * e_im, low_masks))
            lefts_im.append(spread(w_re * e_im + w_im * e_re, low_masks))
            rights.append((w_re * f_re - w_im * f_im, w_re * f_im + w_im * f_re))
            highs.append(jnp.broadcast_to(high, (SIDE, LANES)))
            masks_high.append(masks_of(high))
        a_re = jnp.concatenate(lefts_re, axis=1)
        a_im = jnp.concatenate(lefts_im, axis=1)
        y_re = jnp.dot(left, a_re, preferred_element_type=F32)
        y_im = jnp.dot(left, a_im, preferred_element_type=F32)

        def chosen(y, t):
            y = y[:, t * LANES : (t + 1) * LANES]
            y = y[: 4 * SIDE] + y[4 * SIDE :]
            parts = [y[k * SIDE : (k + 1) * SIDE] for k in range(4)]
            upper = jnp.where(highs[t] == 3, parts[3], parts[2])
            lower = jnp.where(highs[t] == 1, parts[1], parts[0])
            return jnp.where(highs[t] >= 2, upper, lower)

        z_re_all, z_im_all = [], []
        for t in range(per_chunk):
            row = first + t
            b_re, b_im = rights[t]
            p_re, p_im = chosen(y_re, t), chosen(y_im, t)
            pred_re = jnp.sum(p_re * b_re - p_im * b_im, axis=0, keepdims=True)
            pred_im = jnp.sum(p_re * b_im + p_im * b_re, axis=0, keepdims=True)
            weight = weight_ref[pl.ds(row, 1), :]
            r_re = weight * (data_ref[0, pl.ds(row, 1), :] - pred_re)
            r_im = weight * (data_ref[1, pl.ds(row, 1), :] - pred_im)
            residual_ref[0, pl.ds(row, 1), :] = r_re
            residual_ref[1, pl.ds(row, 1), :] = r_im
            z_re_all.append(spread(r_re * b_re + r_im * b_im, masks_high[t]))
            z_im_all.append(spread(r_im * b_re - r_re * b_im, masks_high[t]))

        def crossed(x, y):
            return lax.dot_general(
                x, y, (((1,), (1,)), ((), ())), preferred_element_type=F32
            )

        return crossed(jnp.concatenate(z_re_all, axis=1), a_re) + crossed(
            jnp.concatenate(z_im_all, axis=1), a_im
        )

    total = None
    for first in range(0, rows, per_chunk):
        more = one_chunk(first)
        total = more if total is None else total + more
    total = total.T
    total = total[:, : 4 * SIDE] + total[:, 4 * SIDE :]
    grid_ref[...] = total[: 4 * SIDE] + total[4 * SIDE :]
    for low in range(4):
        parts = [grid_ref[pl.ds(low * SIDE + s, 8, stride=4), :] for s in range(4)]
        for high in range(4):
            dirty_ref[pl.ds(high * 4 + low, 8, stride=SLOTS), :] = jnp.concatenate(
                [p[:, high * SIDE : (high + 1) * SIDE] for p in parts], axis=1
            )


def visibilities(image, table, slot, plane, offset, data, weight):
    rows = slot.shape[0]
    return pl.pallas_call(
        visibility_kernel,
        out_shape=(
            jax.ShapeDtypeStruct((2, rows, LANES), F32),
            jax.ShapeDtypeStruct((CHANS * SLOTS, LANES), F32),
        ),
        in_specs=[pl.BlockSpec(memory_space=pltpu.VMEM)] * 8,
        out_specs=(pl.BlockSpec(memory_space=pltpu.VMEM),) * 2,
        scratch_shapes=[
            pltpu.VMEM((LANES, LANES), F32),
        ],
        compiler_params=pltpu.CompilerParams(vmem_limit_bytes=24 * 1024 * 1024),
        name="visibilities",
    )(image, table, jnp.asarray(phase_tables()), slot, plane, offset, data, weight)


def select_kernel(list_ref, model_ref, taps_ref, phase_ref, image_ref, table_ref):
    scale = 1.0 / math.sqrt(SIDE)
    cos_s = phase_ref[0] * scale
    sin_s = phase_ref[1] * scale

    def tapped(table, taps):
        return jnp.dot(
            table, taps, precision=lax.Precision.HIGHEST, preferred_element_type=F32
        )

    k_re = tapped(cos_s, taps_ref[0]) - tapped(sin_s, taps_ref[1])
    k_im = tapped(cos_s, taps_ref[1]) + tapped(sin_s, taps_ref[0])
    table_ref[0] = jnp.concatenate([k_re] * 4, axis=1)
    table_ref[1] = jnp.concatenate([k_im] * 4, axis=1)
    for channel in range(CHANS):
        offset = (channel - 0.5 * (CHANS - 1)) / CHANS
        for slot in range(SLOTS):
            tile = list_ref[channel, slot]
            first = (tile // WITHIN) * (2 * WITHIN) + tile % WITHIN
            image_ref[pl.ds(channel * SLOTS + slot, 1), :] = model_ref[
                pl.ds(first, 1), :
            ] + offset * model_ref[pl.ds(first + WITHIN, 1), :]


def select(listed, model, taps):
    return pl.pallas_call(
        select_kernel,
        out_shape=(
            jax.ShapeDtypeStruct((CHANS * SLOTS, LANES), F32),
            jax.ShapeDtypeStruct((2, SIDE, LANES), F32),
        ),
        in_specs=[
            pl.BlockSpec(memory_space=pltpu.SMEM),
            *[pl.BlockSpec(memory_space=pltpu.VMEM)] * 3,
        ],
        out_specs=(pl.BlockSpec(memory_space=pltpu.VMEM),) * 2,
        compiler_params=pltpu.CompilerParams(vmem_limit_bytes=8 * 1024 * 1024),
        name="select",
    )(listed, model, taps, jnp.asarray(phase_tables()[:, :, :8]))


def collect_kernel(list_ref, dirty_ref, owned_ref):
    owned_ref[...] = jnp.zeros_like(owned_ref)
    for channel in range(CHANS):
        offset = (channel - 0.5 * (CHANS - 1)) / CHANS
        for slot in range(SLOTS):
            tile = list_ref[channel, slot]
            first = (tile // WITHIN) * (2 * WITHIN) + tile % WITHIN
            row = dirty_ref[pl.ds(channel * SLOTS + slot, 1), :]
            owned_ref[pl.ds(first, 1), :] += row
            owned_ref[pl.ds(first + WITHIN, 1), :] += offset * row


def collect(listed, dirty):
    return pl.pallas_call(
        collect_kernel,
        out_shape=jax.ShapeDtypeStruct((OWNERS * 2 * WITHIN, LANES), F32),
        in_specs=[
            pl.BlockSpec(memory_space=pltpu.SMEM),
            pl.BlockSpec(memory_space=pltpu.VMEM),
        ],
        out_specs=pl.BlockSpec(memory_space=pltpu.VMEM),
        compiler_params=pltpu.CompilerParams(vmem_limit_bytes=8 * 1024 * 1024),
        name="collect",
    )(listed, dirty)


def finish_kernel(parts_ref, step_ref):
    offsets = (np.arange(CHANS) - 0.5 * (CHANS - 1)) / CHANS
    total = jnp.sum(parts_ref[...], axis=0)
    step_ref[0] = total[:WITHIN] * (1.0 / CHANS)
    step_ref[1] = total[WITHIN:] * float(1.0 / np.sum(offsets * offsets))


def finish(parts):
    return pl.pallas_call(
        finish_kernel,
        out_shape=jax.ShapeDtypeStruct((2, WITHIN, LANES), F32),
        in_specs=[pl.BlockSpec(memory_space=pltpu.VMEM)],
        out_specs=pl.BlockSpec(memory_space=pltpu.VMEM),
        compiler_params=pltpu.CompilerParams(vmem_limit_bytes=8 * 1024 * 1024),
        name="finish",
    )(parts)


def shards(model, kernels, vis_data, vis_weight, tile_list, vis_slot, vis_wplane, vis_offset):
    count = vis_weight.shape[1]
    rows = count // LANES
    with jax.named_scope("lists"):
        listed = lax.all_gather(tile_list.reshape(1, SLOTS), "chan", axis=0, tiled=True)
    with jax.named_scope("spread_model"):
        own = model.reshape(1, 2 * WITHIN, LANES)
        every = lax.all_to_all(
            jnp.broadcast_to(own, (OWNERS, 2 * WITHIN, LANES)), "vis", 0, 0, tiled=True
        )
    chosen, table = select(
        listed, every.reshape(OWNERS * 2 * WITHIN, LANES), kernels.transpose(0, 2, 1)
    )
    with jax.named_scope("images"):
        image = lax.all_to_all(chosen, "chan", 0, 0, tiled=True)
    residual, dirty = visibilities(
        image,
        table,
        vis_slot.reshape(rows, LANES),
        vis_wplane.reshape(rows, LANES),
        vis_offset.reshape(2, rows, LANES),
        vis_data.reshape(2, rows, LANES),
        vis_weight.reshape(rows, LANES),
    )
    with jax.named_scope("dirty_cells"):
        pieces = lax.all_to_all(dirty, "chan", 0, 0, tiled=True)
    owned = collect(listed, pieces)
    with jax.named_scope("owners"):
        summed = lax.all_to_all(
            owned.reshape(OWNERS, 2 * WITHIN, LANES), "vis", 0, 0, tiled=True
        )
    model_step = finish(summed)
    return (model_step, residual.reshape(2, 1, count))


def solution(mesh):
    placed = (
        P(None, "vis", "chan"),
        P(),
        P(None, "chan", "vis"),
        P("chan", "vis"),
        P("chan", "vis", None),
        P("chan", "vis"),
        P("chan", "vis"),
        P(None, "chan", "vis"),
    )
    return jax.shard_map(
        shards,
        mesh=mesh,
        in_specs=placed,
        out_specs=(P(None, "vis", "chan"), P(None, "chan", "vis")),
        check_vma=False,
    )
```

```python
import math

import jax
import jax.numpy as jnp
import numpy as np
from jax import lax
from jax.experimental import pallas as pl
from jax.experimental.pallas import tpu as pltpu
from jax.sharding import PartitionSpec as P

SIDE = 32
LANES = 128
SLOTS = 16
OWNERS = 64
CHANS = 8
WITHIN = 4
CHUNK = 512

F32 = jnp.float32
BF16 = jnp.bfloat16


def phase_tables():
    index = np.arange(SIDE)
    turn = np.zeros((SIDE, LANES), np.int64)
    turn[:, :SIDE] = index[:, None] * index[None, :] % SIDE
    angle = 2.0 * np.pi / SIDE * turn
    return np.stack([np.cos(angle), -np.sin(angle)]).astype(np.float32)


def split(x):
    high = x.astype(BF16)
    return high, (x - high.astype(F32)).astype(BF16)


def visibility_kernel(
    image_ref, table_ref, phase_ref, slot_ref, plane_ref, offset_ref, data_ref, weight_ref,
    residual_ref, dirty_ref, grid_ref,
):
    rows = slot_ref.shape[0]
    for low in range(4):
        tiles = [image_ref[pl.ds(high * 4 + low, 8, stride=SLOTS), :] for high in range(4)]
        for step in range(4):
            grid_ref[pl.ds(low * SIDE + step, 8, stride=4), :] = jnp.concatenate(
                [t[:, step * SIDE : (step + 1) * SIDE] for t in tiles], axis=1
            )
    turned = grid_ref[...].T
    t_high, t_low = split(turned)
    left = jnp.concatenate(
        [jnp.concatenate([t_high, t_high], axis=1), jnp.concatenate([t_low, t_low], axis=1)],
        axis=0,
    )

    def spread(x, masks):
        high, low = split(x)
        return jnp.concatenate([high * m for m in masks] + [low * m for m in masks], axis=0)

    def masks_of(part):
        return [
            jnp.broadcast_to(jnp.where(part == k, F32(1), F32(0)), (SIDE, LANES)).astype(BF16)
            for k in range(4)
        ]

    def take(table, index):
        return jnp.take_along_axis(table, index, axis=1, mode="promise_in_bounds")

    per_chunk = CHUNK // LANES

    def one_chunk(first):
        lefts_re, lefts_im, rights, masks_high, highs = [], [], [], [], []
        for t in range(per_chunk):
            row = first + t
            slot = slot_ref[pl.ds(row, 1), :]
            plane = jnp.broadcast_to(plane_ref[pl.ds(row, 1), :], (SIDE, LANES))
            u0 = jnp.broadcast_to(offset_ref[0, pl.ds(row, 1), :], (SIDE, LANES))
            v0 = jnp.broadcast_to(offset_ref[1, pl.ds(row, 1), :], (SIDE, LANES))
            w_re, w_im = take(table_ref[0], plane), take(table_ref[1], plane)
            e_re, e_im = take(phase_ref[0], u0), take(phase_ref[1], u0)
            f_re, f_im = take(phase_ref[0], v0), take(phase_ref[1], v0)
            low_masks = masks_of(slot & 3)
            high = slot >> 2
            lefts_re.append(spread(w_re * e_re - w_im * e_im, low_masks))
            lefts_im.append(spread(w_re * e_im + w_im * e_re, low_masks))
            rights.append((w_re * f_re - w_im * f_im, w_re * f_im + w_im * f_re))
            highs.append(jnp.broadcast_to(high, (SIDE, LANES)))
            masks_high.append(masks_of(high))
        a_re = jnp.concatenate(lefts_re, axis=1)
        a_im = jnp.concatenate(lefts_im, axis=1)
        y_re = jnp.dot(left, a_re, preferred_element_type=F32)
        y_im = jnp.dot(left, a_im, preferred_element_type=F32)

        def chosen(y, t):
            y = y[:, t * LANES : (t + 1) * LANES]
            y = y[: 4 * SIDE] + y[4 * SIDE :]
            parts = [y[k * SIDE : (k + 1) * SIDE] for k in range(4)]
            upper = jnp.where(highs[t] == 3, parts[3], parts[2])
            lower = jnp.where(highs[t] == 1, parts[1], parts[0])
            return jnp.where(highs[t] >= 2, upper, lower)

        z_re_all, z_im_all = [], []
        for t in range(per_chunk):
            row = first + t
            b_re, b_im = rights[t]
            p_re, p_im = chosen(y_re, t), chosen(y_im, t)
            pred_re = jnp.sum(p_re * b_re - p_im * b_im, axis=0, keepdims=True)
            pred_im = jnp.sum(p_re * b_im + p_im * b_re, axis=0, keepdims=True)
            weight = weight_ref[pl.ds(row, 1), :]
            r_re = weight * (data_ref[0, pl.ds(row, 1), :] - pred_re)
            r_im = weight * (data_ref[1, pl.ds(row, 1), :] - pred_im)
            residual_ref[0, pl.ds(row, 1), :] = r_re
            residual_ref[1, pl.ds(row, 1), :] = r_im
            z_re_all.append(spread(r_re * b_re + r_im * b_im, masks_high[t]))
            z_im_all.append(spread(r_im * b_re - r_re * b_im, masks_high[t]))

        def crossed(x, y):
            return lax.dot_general(
                x, y, (((1,), (1,)), ((), ())), preferred_element_type=F32
            )

        return crossed(jnp.concatenate(z_re_all, axis=1), a_re) + crossed(
            jnp.concatenate(z_im_all, axis=1), a_im
        )

    total = None
    for first in range(0, rows, per_chunk):
        more = one_chunk(first)
        total = more if total is None else total + more
    total = total.T
    total = total[:, : 4 * SIDE] + total[:, 4 * SIDE :]
    grid_ref[...] = total[: 4 * SIDE] + total[4 * SIDE :]
    for low in range(4):
        parts = [grid_ref[pl.ds(low * SIDE + s, 8, stride=4), :] for s in range(4)]
        for high in range(4):
            dirty_ref[pl.ds(high * 4 + low, 8, stride=SLOTS), :] = jnp.concatenate(
                [p[:, high * SIDE : (high + 1) * SIDE] for p in parts], axis=1
            )


def visibilities(image, table, slot, plane, offset, data, weight):
    rows = slot.shape[0]
    return pl.pallas_call(
        visibility_kernel,
        out_shape=(
            jax.ShapeDtypeStruct((2, rows, LANES), F32),
            jax.ShapeDtypeStruct((CHANS * SLOTS, LANES), F32),
        ),
        in_specs=[pl.BlockSpec(memory_space=pltpu.VMEM)] * 8,
        out_specs=(pl.BlockSpec(memory_space=pltpu.VMEM),) * 2,
        scratch_shapes=[
            pltpu.VMEM((LANES, LANES), F32),
        ],
        compiler_params=pltpu.CompilerParams(vmem_limit_bytes=24 * 1024 * 1024),
        name="visibilities",
    )(image, table, jnp.asarray(phase_tables()), slot, plane, offset, data, weight)


def select_kernel(list_ref, model_ref, taps_ref, phase_ref, image_ref, table_ref):
    scale = 1.0 / math.sqrt(SIDE)
    cos_s = phase_ref[0] * scale
    sin_s = phase_ref[1] * scale

    def tapped(table, taps):
        return jnp.dot(
            table, taps, precision=lax.Precision.HIGHEST, preferred_element_type=F32
        )

    k_re = tapped(cos_s, taps_ref[0]) - tapped(sin_s, taps_ref[1])
    k_im = tapped(cos_s, taps_ref[1]) + tapped(sin_s, taps_ref[0])
    table_ref[0] = jnp.concatenate([k_re] * 4, axis=1)
    table_ref[1] = jnp.concatenate([k_im] * 4, axis=1)
    for channel in range(CHANS):
        offset = (channel - 0.5 * (CHANS - 1)) / CHANS
        for slot in range(SLOTS):
            tile = list_ref[channel, slot]
            first = 2 * tile - (tile & (WITHIN - 1))
            image_ref[pl.ds(channel * SLOTS + slot, 1), :] = model_ref[
                pl.ds(first, 1), :
            ] + offset * model_ref[pl.ds(first + WITHIN, 1), :]


def select(listed, model, taps):
    return pl.pallas_call(
        select_kernel,
        out_shape=(
            jax.ShapeDtypeStruct((CHANS * SLOTS, LANES), F32),
            jax.ShapeDtypeStruct((2, SIDE, LANES), F32),
        ),
        in_specs=[
            pl.BlockSpec(memory_space=pltpu.SMEM),
            *[pl.BlockSpec(memory_space=pltpu.VMEM)] * 3,
        ],
        out_specs=(pl.BlockSpec(memory_space=pltpu.VMEM),) * 2,
        compiler_params=pltpu.CompilerParams(vmem_limit_bytes=8 * 1024 * 1024),
        name="select",
    )(listed, model, taps, jnp.asarray(phase_tables()[:, :, :8]))


def collect_kernel(list_ref, dirty_ref, owned_ref):
    owned_ref[...] = jnp.zeros_like(owned_ref)
    for channel in range(CHANS):
        offset = (channel - 0.5 * (CHANS - 1)) / CHANS
        firsts = []
        for slot in range(SLOTS):
            tile = list_ref[channel, slot]
            firsts.append(2 * tile - (tile & (WITHIN - 1)))
        rows = [dirty_ref[pl.ds(channel * SLOTS + slot, 1), :] for slot in range(SLOTS)]
        zeros = [owned_ref[pl.ds(first, 1), :] for first in firsts]
        ones = [owned_ref[pl.ds(first + WITHIN, 1), :] for first in firsts]
        for first, row, zero, one in zip(firsts, rows, zeros, ones):
            owned_ref[pl.ds(first, 1), :] = zero + row
            owned_ref[pl.ds(first + WITHIN, 1), :] = one + offset * row


def collect(listed, dirty):
    return pl.pallas_call(
        collect_kernel,
        out_shape=jax.ShapeDtypeStruct((OWNERS * 2 * WITHIN, LANES), F32),
        in_specs=[
            pl.BlockSpec(memory_space=pltpu.SMEM),
            pl.BlockSpec(memory_space=pltpu.VMEM),
        ],
        out_specs=pl.BlockSpec(memory_space=pltpu.VMEM),
        compiler_params=pltpu.CompilerParams(vmem_limit_bytes=8 * 1024 * 1024),
        name="collect",
    )(listed, dirty)


def finish_kernel(parts_ref, step_ref):
    offsets = (np.arange(CHANS) - 0.5 * (CHANS - 1)) / CHANS
    total = jnp.sum(parts_ref[...], axis=0)
    step_ref[0] = total[:WITHIN] * (1.0 / CHANS)
    step_ref[1] = total[WITHIN:] * float(1.0 / np.sum(offsets * offsets))


def finish(parts):
    return pl.pallas_call(
        finish_kernel,
        out_shape=jax.ShapeDtypeStruct((2, WITHIN, LANES), F32),
        in_specs=[pl.BlockSpec(memory_space=pltpu.VMEM)],
        out_specs=pl.BlockSpec(memory_space=pltpu.VMEM),
        compiler_params=pltpu.CompilerParams(vmem_limit_bytes=8 * 1024 * 1024),
        name="finish",
    )(parts)


def shards(model, kernels, vis_data, vis_weight, tile_list, vis_slot, vis_wplane, vis_offset):
    count = vis_weight.shape[1]
    rows = count // LANES
    with jax.named_scope("lists"):
        listed = lax.all_gather(tile_list.reshape(1, SLOTS), "chan", axis=0, tiled=True)
    with jax.named_scope("spread_model"):
        own = model.reshape(1, 2 * WITHIN, LANES)
        every = lax.all_to_all(
            jnp.broadcast_to(own, (OWNERS, 2 * WITHIN, LANES)), "vis", 0, 0, tiled=True
        )
    chosen, table = select(
        listed, every.reshape(OWNERS * 2 * WITHIN, LANES), kernels.transpose(0, 2, 1)
    )
    with jax.named_scope("images"):
        image = lax.all_to_all(chosen, "chan", 0, 0, tiled=True)
    residual, dirty = visibilities(
        image,
        table,
        vis_slot.reshape(rows, LANES),
        vis_wplane.reshape(rows, LANES),
        vis_offset.reshape(2, rows, LANES),
        vis_data.reshape(2, rows, LANES),
        vis_weight.reshape(rows, LANES),
    )
    with jax.named_scope("dirty_cells"):
        pieces = lax.all_to_all(dirty, "chan", 0, 0, tiled=True)
    owned = collect(listed, pieces)
    with jax.named_scope("owners"):
        summed = lax.all_to_all(
            owned.reshape(OWNERS, 2 * WITHIN, LANES), "vis", 0, 0, tiled=True
        )
    model_step = finish(summed)
    return (model_step, residual.reshape(2, 1, count))


def solution(mesh):
    placed = (
        P(None, "vis", "chan"),
        P(),
        P(None, "chan", "vis"),
        P("chan", "vis"),
        P("chan", "vis", None),
        P("chan", "vis"),
        P("chan", "vis"),
        P(None, "chan", "vis"),
    )
    return jax.shard_map(
        shards,
        mesh=mesh,
        in_specs=placed,
        out_specs=(P(None, "vis", "chan"), P(None, "chan", "vis")),
        check_vma=False,
    )
```

```python
import math

import jax
import jax.numpy as jnp
import numpy as np
from jax import lax
from jax.experimental import pallas as pl
from jax.experimental.pallas import tpu as pltpu
from jax.sharding import PartitionSpec as P

SIDE = 32
LANES = 128
SLOTS = 16
OWNERS = 64
CHANS = 8
WITHIN = 4
CHUNK = 512

F32 = jnp.float32
BF16 = jnp.bfloat16


def phase_tables():
    index = np.arange(SIDE)
    turn = np.zeros((SIDE, LANES), np.int64)
    turn[:, :SIDE] = index[:, None] * index[None, :] % SIDE
    angle = 2.0 * np.pi / SIDE * turn
    return np.stack([np.cos(angle), -np.sin(angle)]).astype(np.float32)


def split(x):
    high = x.astype(BF16)
    return high, (x - high.astype(F32)).astype(BF16)


def visibility_kernel(
    image_ref, table_ref, phase_ref, slot_ref, plane_ref, offset_ref, data_ref, weight_ref,
    residual_ref, dirty_ref, grid_ref,
):
    rows = slot_ref.shape[0]
    for low in range(4):
        tiles = [image_ref[pl.ds(high * 4 + low, 8, stride=SLOTS), :] for high in range(4)]
        for step in range(4):
            grid_ref[pl.ds(low * SIDE + step, 8, stride=4), :] = jnp.concatenate(
                [t[:, step * SIDE : (step + 1) * SIDE] for t in tiles], axis=1
            )
    turned = grid_ref[...].T
    t_high, t_low = split(turned)
    left = jnp.concatenate(
        [jnp.concatenate([t_high, t_high], axis=1), jnp.concatenate([t_low, t_low], axis=1)],
        axis=0,
    )

    def spread(x, masks):
        high, low = split(x)
        return jnp.concatenate([high * m for m in masks] + [low * m for m in masks], axis=0)

    def masks_of(part):
        return [
            jnp.broadcast_to(jnp.where(part == k, F32(1), F32(0)), (SIDE, LANES)).astype(BF16)
            for k in range(4)
        ]

    def take(table, index):
        return jnp.take_along_axis(table, index, axis=1, mode="promise_in_bounds")

    per_chunk = CHUNK // LANES

    def one_chunk(first):
        lefts_re, lefts_im, rights, masks_high, highs = [], [], [], [], []
        for t in range(per_chunk):
            row = first + t
            slot = slot_ref[pl.ds(row, 1), :]
            plane = jnp.broadcast_to(plane_ref[pl.ds(row, 1), :], (SIDE, LANES))
            u0 = jnp.broadcast_to(offset_ref[0, pl.ds(row, 1), :], (SIDE, LANES))
            v0 = jnp.broadcast_to(offset_ref[1, pl.ds(row, 1), :], (SIDE, LANES))
            w_re, w_im = take(table_ref[0], plane), take(table_ref[1], plane)
            e_re, e_im = take(phase_ref[0], u0), take(phase_ref[1], u0)
            f_re, f_im = take(phase_ref[0], v0), take(phase_ref[1], v0)
            low_masks = masks_of(slot & 3)
            high = slot >> 2
            lefts_re.append(spread(w_re * e_re - w_im * e_im, low_masks))
            lefts_im.append(spread(w_re * e_im + w_im * e_re, low_masks))
            rights.append((w_re * f_re - w_im * f_im, w_re * f_im + w_im * f_re))
            highs.append(jnp.broadcast_to(high, (SIDE, LANES)))
            masks_high.append(masks_of(high))
        a_re = jnp.concatenate(lefts_re, axis=1)
        a_im = jnp.concatenate(lefts_im, axis=1)
        y_re = jnp.dot(left, a_re, preferred_element_type=F32)
        y_im = jnp.dot(left, a_im, preferred_element_type=F32)

        def chosen(y, t):
            y = y[:, t * LANES : (t + 1) * LANES]
            y = y[: 4 * SIDE] + y[4 * SIDE :]
            parts = [y[k * SIDE : (k + 1) * SIDE] for k in range(4)]
            upper = jnp.where(highs[t] == 3, parts[3], parts[2])
            lower = jnp.where(highs[t] == 1, parts[1], parts[0])
            return jnp.where(highs[t] >= 2, upper, lower)

        z_re_all, z_im_all = [], []
        for t in range(per_chunk):
            row = first + t
            b_re, b_im = rights[t]
            p_re, p_im = chosen(y_re, t), chosen(y_im, t)
            pred_re = jnp.sum(p_re * b_re - p_im * b_im, axis=0, keepdims=True)
            pred_im = jnp.sum(p_re * b_im + p_im * b_re, axis=0, keepdims=True)
            weight = weight_ref[pl.ds(row, 1), :]
            r_re = weight * (data_ref[0, pl.ds(row, 1), :] - pred_re)
            r_im = weight * (data_ref[1, pl.ds(row, 1), :] - pred_im)
            residual_ref[0, pl.ds(row, 1), :] = r_re
            residual_ref[1, pl.ds(row, 1), :] = r_im
            z_re_all.append(spread(r_re * b_re + r_im * b_im, masks_high[t]))
            z_im_all.append(spread(r_im * b_re - r_re * b_im, masks_high[t]))

        def crossed(x, y):
            return lax.dot_general(
                x, y, (((1,), (1,)), ((), ())), preferred_element_type=F32
            )

        return crossed(jnp.concatenate(z_re_all, axis=1), a_re) + crossed(
            jnp.concatenate(z_im_all, axis=1), a_im
        )

    total = None
    for first in range(0, rows, per_chunk):
        more = one_chunk(first)
        total = more if total is None else total + more
    total = total[:, : 4 * SIDE] + total[:, 4 * SIDE :]
    grid_ref[...] = (total[: 4 * SIDE] + total[4 * SIDE :]).T
    for low in range(4):
        parts = [grid_ref[pl.ds(low * SIDE + s, 8, stride=4), :] for s in range(4)]
        for high in range(4):
            dirty_ref[pl.ds(high * 4 + low, 8, stride=SLOTS), :] = jnp.concatenate(
                [p[:, high * SIDE : (high + 1) * SIDE] for p in parts], axis=1
            )


def visibilities(image, table, slot, plane, offset, data, weight):
    rows = slot.shape[0]
    return pl.pallas_call(
        visibility_kernel,
        out_shape=(
            jax.ShapeDtypeStruct((2, rows, LANES), F32),
            jax.ShapeDtypeStruct((CHANS * SLOTS, LANES), F32),
        ),
        in_specs=[pl.BlockSpec(memory_space=pltpu.VMEM)] * 8,
        out_specs=(pl.BlockSpec(memory_space=pltpu.VMEM),) * 2,
        scratch_shapes=[
            pltpu.VMEM((LANES, LANES), F32),
        ],
        compiler_params=pltpu.CompilerParams(vmem_limit_bytes=24 * 1024 * 1024),
        name="visibilities",
    )(image, table, jnp.asarray(phase_tables()), slot, plane, offset, data, weight)


def select_kernel(list_ref, model_ref, taps_ref, phase_ref, image_ref, table_ref):
    scale = 1.0 / math.sqrt(SIDE)
    cos_s = phase_ref[0] * scale
    sin_s = phase_ref[1] * scale

    def tapped(table, taps):
        return jnp.dot(
            table, taps, precision=lax.Precision.HIGHEST, preferred_element_type=F32
        )

    k_re = tapped(cos_s, taps_ref[0]) - tapped(sin_s, taps_ref[1])
    k_im = tapped(cos_s, taps_ref[1]) + tapped(sin_s, taps_ref[0])
    table_ref[0] = jnp.concatenate([k_re] * 4, axis=1)
    table_ref[1] = jnp.concatenate([k_im] * 4, axis=1)
    for channel in range(CHANS):
        offset = (channel - 0.5 * (CHANS - 1)) / CHANS
        for slot in range(SLOTS):
            tile = list_ref[channel, slot]
            first = 2 * tile - (tile & (WITHIN - 1))
            image_ref[pl.ds(channel * SLOTS + slot, 1), :] = model_ref[
                pl.ds(first, 1), :
            ] + offset * model_ref[pl.ds(first + WITHIN, 1), :]


def select(listed, model, taps):
    return pl.pallas_call(
        select_kernel,
        out_shape=(
            jax.ShapeDtypeStruct((CHANS * SLOTS, LANES), F32),
            jax.ShapeDtypeStruct((2, SIDE, LANES), F32),
        ),
        in_specs=[
            pl.BlockSpec(memory_space=pltpu.SMEM),
            *[pl.BlockSpec(memory_space=pltpu.VMEM)] * 3,
        ],
        out_specs=(pl.BlockSpec(memory_space=pltpu.VMEM),) * 2,
        compiler_params=pltpu.CompilerParams(vmem_limit_bytes=8 * 1024 * 1024),
        name="select",
    )(listed, model, taps, jnp.asarray(phase_tables()[:, :, :8]))


def collect_kernel(list_ref, dirty_ref, owned_ref):
    owned_ref[...] = jnp.zeros_like(owned_ref)
    for channel in range(CHANS):
        offset = (channel - 0.5 * (CHANS - 1)) / CHANS
        firsts = []
        for slot in range(SLOTS):
            tile = list_ref[channel, slot]
            firsts.append(2 * tile - (tile & (WITHIN - 1)))
        rows = [dirty_ref[pl.ds(channel * SLOTS + slot, 1), :] for slot in range(SLOTS)]
        zeros = [owned_ref[pl.ds(first, 1), :] for first in firsts]
        ones = [owned_ref[pl.ds(first + WITHIN, 1), :] for first in firsts]
        for first, row, zero, one in zip(firsts, rows, zeros, ones):
            owned_ref[pl.ds(first, 1), :] = zero + row
            owned_ref[pl.ds(first + WITHIN, 1), :] = one + offset * row


def collect(listed, dirty):
    return pl.pallas_call(
        collect_kernel,
        out_shape=jax.ShapeDtypeStruct((OWNERS * 2 * WITHIN, LANES), F32),
        in_specs=[
            pl.BlockSpec(memory_space=pltpu.SMEM),
            pl.BlockSpec(memory_space=pltpu.VMEM),
        ],
        out_specs=pl.BlockSpec(memory_space=pltpu.VMEM),
        compiler_params=pltpu.CompilerParams(vmem_limit_bytes=8 * 1024 * 1024),
        name="collect",
    )(listed, dirty)


def finish_kernel(parts_ref, step_ref):
    offsets = (np.arange(CHANS) - 0.5 * (CHANS - 1)) / CHANS
    total = jnp.sum(parts_ref[...], axis=0)
    step_ref[0] = total[:WITHIN] * (1.0 / CHANS)
    step_ref[1] = total[WITHIN:] * float(1.0 / np.sum(offsets * offsets))


def finish(parts):
    return pl.pallas_call(
        finish_kernel,
        out_shape=jax.ShapeDtypeStruct((2, WITHIN, LANES), F32),
        in_specs=[pl.BlockSpec(memory_space=pltpu.VMEM)],
        out_specs=pl.BlockSpec(memory_space=pltpu.VMEM),
        compiler_params=pltpu.CompilerParams(vmem_limit_bytes=8 * 1024 * 1024),
        name="finish",
    )(parts)


def shards(model, kernels, vis_data, vis_weight, tile_list, vis_slot, vis_wplane, vis_offset):
    count = vis_weight.shape[1]
    rows = count // LANES
    with jax.named_scope("lists"):
        listed = lax.all_gather(tile_list.reshape(1, SLOTS), "chan", axis=0, tiled=True)
    with jax.named_scope("spread_model"):
        own = model.reshape(1, 2 * WITHIN, LANES)
        every = lax.all_to_all(
            jnp.broadcast_to(own, (OWNERS, 2 * WITHIN, LANES)), "vis", 0, 0, tiled=True
        )
    chosen, table = select(
        listed, every.reshape(OWNERS * 2 * WITHIN, LANES), kernels.transpose(0, 2, 1)
    )
    with jax.named_scope("images"):
        image = lax.all_to_all(chosen, "chan", 0, 0, tiled=True)
    residual, dirty = visibilities(
        image,
        table,
        vis_slot.reshape(rows, LANES),
        vis_wplane.reshape(rows, LANES),
        vis_offset.reshape(2, rows, LANES),
        vis_data.reshape(2, rows, LANES),
        vis_weight.reshape(rows, LANES),
    )
    with jax.named_scope("dirty_cells"):
        pieces = lax.all_to_all(dirty, "chan", 0, 0, tiled=True)
    owned = collect(listed, pieces)
    with jax.named_scope("owners"):
        summed = lax.all_to_all(
            owned.reshape(OWNERS, 2 * WITHIN, LANES), "vis", 0, 0, tiled=True
        )
    model_step = finish(summed)
    return (model_step, residual.reshape(2, 1, count))


def solution(mesh):
    placed = (
        P(None, "vis", "chan"),
        P(),
        P(None, "chan", "vis"),
        P("chan", "vis"),
        P("chan", "vis", None),
        P("chan", "vis"),
        P("chan", "vis"),
        P(None, "chan", "vis"),
    )
    return jax.shard_map(
        shards,
        mesh=mesh,
        in_specs=placed,
        out_specs=(P(None, "vis", "chan"), P(None, "chan", "vis")),
        check_vma=False,
    )
```

```python
import math

import jax
import jax.numpy as jnp
import numpy as np
from jax import lax
from jax.experimental import pallas as pl
from jax.experimental.pallas import tpu as pltpu
from jax.sharding import PartitionSpec as P

SIDE = 32
LANES = 128
SLOTS = 16
OWNERS = 64
CHANS = 8
WITHIN = 4
CHUNK = 512

F32 = jnp.float32
BF16 = jnp.bfloat16


def phase_tables():
    index = np.arange(SIDE)
    turn = np.zeros((SIDE, LANES), np.int64)
    turn[:, :SIDE] = index[:, None] * index[None, :] % SIDE
    angle = 2.0 * np.pi / SIDE * turn
    return np.stack([np.cos(angle), -np.sin(angle)]).astype(np.float32)


def split(x):
    high = x.astype(BF16)
    return high, (x - high.astype(F32)).astype(BF16)


def visibility_kernel(
    image_ref, table_ref, phase_ref, slot_ref, plane_ref, offset_ref, data_ref, weight_ref,
    residual_ref, dirty_ref, grid_ref,
):
    rows = slot_ref.shape[0]
    for low in range(4):
        tiles = [image_ref[pl.ds(high * 4 + low, 8, stride=SLOTS), :] for high in range(4)]
        for step in range(4):
            grid_ref[pl.ds(low * SIDE + step, 8, stride=4), :] = jnp.concatenate(
                [t[:, step * SIDE : (step + 1) * SIDE] for t in tiles], axis=1
            )
    turned = grid_ref[...].T
    t_high, t_low = split(turned)
    left = jnp.concatenate(
        [jnp.concatenate([t_high, t_high], axis=1), jnp.concatenate([t_low, t_low], axis=1)],
        axis=0,
    )

    def spread(x, masks):
        high, low = split(x)
        return jnp.concatenate([high * m for m in masks] + [low * m for m in masks], axis=0)

    def masks_of(part):
        return [
            jnp.broadcast_to(jnp.where(part == k, F32(1), F32(0)), (SIDE, LANES)).astype(BF16)
            for k in range(4)
        ]

    def take(table, index):
        return jnp.take_along_axis(table, index, axis=1, mode="promise_in_bounds")

    per_chunk = CHUNK // LANES

    def one_chunk(first):
        lefts_re, lefts_im, rights, masks_high, highs = [], [], [], [], []
        for t in range(per_chunk):
            row = first + t
            slot = slot_ref[pl.ds(row, 1), :]
            plane = jnp.broadcast_to(plane_ref[pl.ds(row, 1), :], (SIDE, LANES))
            u0 = jnp.broadcast_to(offset_ref[0, pl.ds(row, 1), :], (SIDE, LANES))
            v0 = jnp.broadcast_to(offset_ref[1, pl.ds(row, 1), :], (SIDE, LANES))
            w_re, w_im = take(table_ref[0], plane), take(table_ref[1], plane)
            e_re, e_im = take(phase_ref[0], u0), take(phase_ref[1], u0)
            f_re, f_im = take(phase_ref[0], v0), take(phase_ref[1], v0)
            low_masks = masks_of(slot & 3)
            high = slot >> 2
            lefts_re.append(spread(w_re * e_re - w_im * e_im, low_masks))
            lefts_im.append(spread(w_re * e_im + w_im * e_re, low_masks))
            rights.append((w_re * f_re - w_im * f_im, w_re * f_im + w_im * f_re))
            highs.append(jnp.broadcast_to(high, (SIDE, LANES)))
            masks_high.append(masks_of(high))
        a_re = jnp.concatenate(lefts_re, axis=1)
        a_im = jnp.concatenate(lefts_im, axis=1)
        y_re = jnp.dot(left, a_re, preferred_element_type=F32)
        y_im = jnp.dot(left, a_im, preferred_element_type=F32)

        def chosen(y, t):
            y = y[:, t * LANES : (t + 1) * LANES]
            y = y[: 4 * SIDE] + y[4 * SIDE :]
            parts = [y[k * SIDE : (k + 1) * SIDE] for k in range(4)]
            upper = jnp.where(highs[t] == 3, parts[3], parts[2])
            lower = jnp.where(highs[t] == 1, parts[1], parts[0])
            return jnp.where(highs[t] >= 2, upper, lower)

        z_re_all, z_im_all = [], []
        for t in range(per_chunk):
            row = first + t
            b_re, b_im = rights[t]
            p_re, p_im = chosen(y_re, t), chosen(y_im, t)
            pred_re = jnp.sum(p_re * b_re - p_im * b_im, axis=0, keepdims=True)
            pred_im = jnp.sum(p_re * b_im + p_im * b_re, axis=0, keepdims=True)
            weight = weight_ref[pl.ds(row, 1), :]
            r_re = weight * (data_ref[0, pl.ds(row, 1), :] - pred_re)
            r_im = weight * (data_ref[1, pl.ds(row, 1), :] - pred_im)
            residual_ref[0, pl.ds(row, 1), :] = r_re
            residual_ref[1, pl.ds(row, 1), :] = r_im
            z_re_all.append(spread(r_re * b_re + r_im * b_im, masks_high[t]))
            z_im_all.append(spread(r_im * b_re - r_re * b_im, masks_high[t]))

        def crossed(x, y):
            return lax.dot_general(
                x, y, (((1,), (1,)), ((), ())), preferred_element_type=F32
            )

        return crossed(jnp.concatenate(z_re_all, axis=1), a_re) + crossed(
            jnp.concatenate(z_im_all, axis=1), a_im
        )

    total = None
    for first in range(0, rows, per_chunk):
        more = one_chunk(first)
        total = more if total is None else total + more
    total = total[:, : 4 * SIDE] + total[:, 4 * SIDE :]
    grid_ref[...] = (total[: 4 * SIDE] + total[4 * SIDE :]).T
    for low in range(4):
        parts = [grid_ref[pl.ds(low * SIDE + s, 8, stride=4), :] for s in range(4)]
        for high in range(4):
            dirty_ref[pl.ds(high * 4 + low, 8, stride=SLOTS), :] = jnp.concatenate(
                [p[:, high * SIDE : (high + 1) * SIDE] for p in parts], axis=1
            )


def visibilities(image, table, slot, plane, offset, data, weight):
    rows = slot.shape[0]
    return pl.pallas_call(
        visibility_kernel,
        out_shape=(
            jax.ShapeDtypeStruct((2, rows, LANES), F32),
            jax.ShapeDtypeStruct((CHANS * SLOTS, LANES), F32),
        ),
        in_specs=[pl.BlockSpec(memory_space=pltpu.VMEM)] * 8,
        out_specs=(pl.BlockSpec(memory_space=pltpu.VMEM),) * 2,
        scratch_shapes=[
            pltpu.VMEM((LANES, LANES), F32),
        ],
        compiler_params=pltpu.CompilerParams(vmem_limit_bytes=24 * 1024 * 1024),
        name="visibilities",
    )(image, table, jnp.asarray(phase_tables()), slot, plane, offset, data, weight)


def select_kernel(list_ref, model_ref, taps_ref, phase_ref, image_ref, table_ref):
    table = jnp.dot(
        phase_ref[...], taps_ref[...],
        precision=lax.Precision.HIGHEST, preferred_element_type=F32,
    )
    k_re, k_im = table[:SIDE], table[SIDE:]
    table_ref[0] = jnp.concatenate([k_re] * 4, axis=1)
    table_ref[1] = jnp.concatenate([k_im] * 4, axis=1)
    for channel in range(CHANS):
        offset = (channel - 0.5 * (CHANS - 1)) / CHANS
        for slot in range(SLOTS):
            tile = list_ref[channel, slot]
            first = 2 * tile - (tile & (WITHIN - 1))
            image_ref[pl.ds(channel * SLOTS + slot, 1), :] = model_ref[
                pl.ds(first, 1), :
            ] + offset * model_ref[pl.ds(first + WITHIN, 1), :]


def select(listed, model, taps):
    cosine, sine = phase_tables()[:, :, :8] / math.sqrt(SIDE)
    turned = np.block([[cosine, -sine], [sine, cosine]]).astype(np.float32)
    return pl.pallas_call(
        select_kernel,
        out_shape=(
            jax.ShapeDtypeStruct((CHANS * SLOTS, LANES), F32),
            jax.ShapeDtypeStruct((2, SIDE, LANES), F32),
        ),
        in_specs=[
            pl.BlockSpec(memory_space=pltpu.SMEM),
            *[pl.BlockSpec(memory_space=pltpu.VMEM)] * 3,
        ],
        out_specs=(pl.BlockSpec(memory_space=pltpu.VMEM),) * 2,
        compiler_params=pltpu.CompilerParams(vmem_limit_bytes=8 * 1024 * 1024),
        name="select",
    )(listed, model, taps, jnp.asarray(turned))


def collect_kernel(list_ref, dirty_ref, owned_ref):
    owned_ref[...] = jnp.zeros_like(owned_ref)
    for channel in range(CHANS):
        offset = (channel - 0.5 * (CHANS - 1)) / CHANS
        firsts = []
        for slot in range(SLOTS):
            tile = list_ref[channel, slot]
            firsts.append(2 * tile - (tile & (WITHIN - 1)))
        rows = [dirty_ref[pl.ds(channel * SLOTS + slot, 1), :] for slot in range(SLOTS)]
        zeros = [owned_ref[pl.ds(first, 1), :] for first in firsts]
        ones = [owned_ref[pl.ds(first + WITHIN, 1), :] for first in firsts]
        for first, row, zero, one in zip(firsts, rows, zeros, ones):
            owned_ref[pl.ds(first, 1), :] = zero + row
            owned_ref[pl.ds(first + WITHIN, 1), :] = one + offset * row


def collect(listed, dirty):
    return pl.pallas_call(
        collect_kernel,
        out_shape=jax.ShapeDtypeStruct((OWNERS * 2 * WITHIN, LANES), F32),
        in_specs=[
            pl.BlockSpec(memory_space=pltpu.SMEM),
            pl.BlockSpec(memory_space=pltpu.VMEM),
        ],
        out_specs=pl.BlockSpec(memory_space=pltpu.VMEM),
        compiler_params=pltpu.CompilerParams(vmem_limit_bytes=8 * 1024 * 1024),
        name="collect",
    )(listed, dirty)


def finish_kernel(parts_ref, step_ref):
    offsets = (np.arange(CHANS) - 0.5 * (CHANS - 1)) / CHANS
    total = jnp.sum(parts_ref[...], axis=0)
    step_ref[0] = total[:WITHIN] * (1.0 / CHANS)
    step_ref[1] = total[WITHIN:] * float(1.0 / np.sum(offsets * offsets))


def finish(parts):
    return pl.pallas_call(
        finish_kernel,
        out_shape=jax.ShapeDtypeStruct((2, WITHIN, LANES), F32),
        in_specs=[pl.BlockSpec(memory_space=pltpu.VMEM)],
        out_specs=pl.BlockSpec(memory_space=pltpu.VMEM),
        compiler_params=pltpu.CompilerParams(vmem_limit_bytes=8 * 1024 * 1024),
        name="finish",
    )(parts)


def shards(model, kernels, vis_data, vis_weight, tile_list, vis_slot, vis_wplane, vis_offset):
    count = vis_weight.shape[1]
    rows = count // LANES
    with jax.named_scope("lists"):
        listed = lax.all_gather(tile_list.reshape(1, SLOTS), "chan", axis=0, tiled=True)
    with jax.named_scope("spread_model"):
        own = model.reshape(1, 2 * WITHIN, LANES)
        every = lax.all_to_all(
            jnp.broadcast_to(own, (OWNERS, 2 * WITHIN, LANES)), "vis", 0, 0, tiled=True
        )
    chosen, table = select(
        listed, every.reshape(OWNERS * 2 * WITHIN, LANES), kernels.transpose(0, 2, 1).reshape(16, SIDE)
    )
    with jax.named_scope("images"):
        image = lax.all_to_all(chosen, "chan", 0, 0, tiled=True)
    residual, dirty = visibilities(
        image,
        table,
        vis_slot.reshape(rows, LANES),
        vis_wplane.reshape(rows, LANES),
        vis_offset.reshape(2, rows, LANES),
        vis_data.reshape(2, rows, LANES),
        vis_weight.reshape(rows, LANES),
    )
    with jax.named_scope("dirty_cells"):
        pieces = lax.all_to_all(dirty, "chan", 0, 0, tiled=True)
    owned = collect(listed, pieces)
    with jax.named_scope("owners"):
        summed = lax.all_to_all(
            owned.reshape(OWNERS, 2 * WITHIN, LANES), "vis", 0, 0, tiled=True
        )
    model_step = finish(summed)
    return (model_step, residual.reshape(2, 1, count))


def solution(mesh):
    placed = (
        P(None, "vis", "chan"),
        P(),
        P(None, "chan", "vis"),
        P("chan", "vis"),
        P("chan", "vis", None),
        P("chan", "vis"),
        P("chan", "vis"),
        P(None, "chan", "vis"),
    )
    return jax.shard_map(
        shards,
        mesh=mesh,
        in_specs=placed,
        out_specs=(P(None, "vis", "chan"), P(None, "chan", "vis")),
        check_vma=False,
    )
```
